256 devices in a mesh: dp: 4 (over y), fsdp: 64 (over z, x, core).
Axes of the slice: x: 4, y: 4, z: 8, core: 2. Of those that a mesh axis runs over, the one named last changes fastest.
Arguments:
- inputs: bfloat16 [90112, 8192], P(('dp', 'fsdp')), may hold values from -6 to 6
- frozen: bfloat16 [8192, 512], P('fsdp'), may hold values from -0.0625 to 0.0625
- cotangent: bfloat16 [90112, 512], P(('dp', 'fsdp')), may hold values from -48 to 48
- delta_slots: bfloat16 [128, 128, 128], P('fsdp'), may hold values from -0.1796875 to 0.1796875
- slot_tile: int32 [128], P('fsdp'), may hold values from -1 to 255, as said below
- token_count: int32 [256], P(('dp', 'fsdp')), may hold values from 1 to 352, as said below
Outputs:
- projected: bfloat16 [90112, 512], P(('dp', 'fsdp'))
- input_grad: bfloat16 [90112, 8192], P(('dp', 'fsdp'))
- delta_grad: float32 [128, 128, 128], P('fsdp')
The draws below stay inside these ranges and needn't reach their ends.
Inputs may be any that keep to these rules, and one draw needn't show every extreme that they name: `slot_tile`: slot s belongs to fsdp index s // 2; an index owns its live blocks in its first slots and empty slots hold -1; live tile numbers are distinct; some index has all 2 slots live and some index has none. `token_count`: some device has all 352 rows valid.
All inputs are finite; a program needn't handle non-finite values.
Results may differ from the reference program's by a relative error of at most 0.0046.
Values may be sent and summed in bfloat16 or wider, within the bound.
No kernel may reach another device: no remote copies, remote signals or barrier semaphores. Data moves between devices by JAX's collectives and lax.ppermute only.
A program may use at most 192 MiB of HBM per device.

```python
import jax
import jax.numpy as jnp
from jax import lax

D = 8192
KV = 512
BLOCK = 128
BLK_DEV = 2
TOK_DEV = 352
SHARDS = 256
TOKENS = 90112
SLOTS = 128
ROW_TILES = 64
COL_TILES = 4
TILES = 256
N_FSDP = 64


def draw_slot_tile(key, part):
    key_a, key_b, key_c = jax.random.split(jax.random.fold_in(key, 17), 3)
    chosen = jax.random.permutation(key_a, TILES)[:SLOTS].astype(jnp.int32)
    level = jax.random.randint(key_b, (N_FSDP,), 0, 10)
    owned = jnp.clip((level - 2) * BLK_DEV // 4, 0, BLK_DEV)
    fullest = jax.random.randint(key_c, (), 0, N_FSDP)
    emptiest = (fullest + 1) % N_FSDP
    owner_ids = jnp.arange(N_FSDP)
    owned = jnp.where(owner_ids == fullest, BLK_DEV, owned)
    owned = jnp.where(owner_ids == emptiest, 0, owned)
    top_slot = fullest * BLK_DEV
    displaced = chosen[top_slot]
    chosen = jnp.where(chosen == TILES - 1, displaced, chosen)
    chosen = jnp.where(jnp.arange(SLOTS) == top_slot, TILES - 1, chosen).astype(jnp.int32)
    slot_rank = jnp.arange(SLOTS) % BLK_DEV
    owner_of = jnp.arange(SLOTS) // BLK_DEV
    return jnp.where(slot_rank < owned[owner_of], chosen, -1).astype(jnp.int32)


def draw_token_count(key, part):
    key_a, key_b = jax.random.split(jax.random.fold_in(key, 29))
    lowest = TOK_DEV // 3
    spread_top = TOK_DEV - lowest - TOK_DEV // 8
    baseline = lowest + spread_top * jnp.arange(SHARDS) // max(SHARDS - 1, 1)
    jitter = jax.random.randint(key_a, (SHARDS,), 0, TOK_DEV // 8 + 1)
    counts = baseline + jitter
    fullest = jax.random.randint(key_b, (), 0, SHARDS)
    counts = jnp.where(jnp.arange(SHARDS) == fullest, TOK_DEV, counts)
    return jnp.clip(counts, 1, TOK_DEV).astype(jnp.int32)


def shard_levels(stream_key, shape, shards, smallest, high):
    def one(position, parts):
        draws = jax.random.uniform(jax.random.fold_in(jax.random.fold_in(stream_key, 6), position), (parts,), jnp.float32, smallest / len(shards), high / len(shards))
        return jnp.repeat(jnp.exp(draws), shape[position] // parts).reshape((-1,) + (1,) * (len(shape) - position - 1))

    gain = one(*shards[0])
    for cut in shards[1:]:
        gain = gain * one(*cut)
    return gain


def normal_values(stream_key, shape, spread, bound, pieces=(), kind=jnp.bfloat16):
    loudness = shard_levels(stream_key, shape, pieces, -0.22, 0.18) if pieces else 1.0
    result = jax.random.normal(stream_key, shape, jnp.float32) * spread * loudness
    return jnp.minimum(jnp.maximum(result, -bound), bound).astype(kind)


def setup_inputs(seed: int = 0) -> dict:
    keys = jax.random.split(jax.random.key(seed), 7)
    return {
        "inputs": normal_values(keys[0], (TOKENS, D), 1.0, 6.0, ((0, 256),)),
        "frozen": normal_values(keys[1], (D, KV), D ** -0.5, 0.0625, ((0, 64),)),
        "cotangent": normal_values(keys[2], (TOKENS, KV), 8.0, 48.0, ((0, 256),)),
        "delta_slots": normal_values(keys[3], (SLOTS, BLOCK, BLOCK), 0.03, 0.1796875, ((0, 64),)),
        "slot_tile": draw_slot_tile(jax.random.fold_in(keys[6], 71), 0),
        "token_count": draw_token_count(jax.random.fold_in(keys[6], 71), 0),
    }


def reference(inputs, frozen, cotangent, delta_slots, slot_tile, token_count):
    tile_count = ROW_TILES * COL_TILES
    slot_target = jnp.where(slot_tile >= 0, slot_tile, tile_count).astype(jnp.int32)
    placed = jnp.zeros((tile_count + 1, BLOCK, BLOCK), jnp.bfloat16).at[slot_target].add(delta_slots)[:tile_count]
    delta_dense = placed.reshape(ROW_TILES, COL_TILES, BLOCK, BLOCK).transpose(0, 2, 1, 3).reshape(D, KV)
    effective = (frozen.astype(jnp.float32) + delta_dense.astype(jnp.float32)).astype(jnp.bfloat16)
    token_total = jnp.sum(token_count).astype(jnp.float32)
    row_ids = jnp.arange(TOK_DEV, dtype=jnp.int32)
    tile_index = jnp.where(slot_tile >= 0, slot_tile, 0).astype(jnp.int32)
    row_tile = (tile_index // COL_TILES).astype(jnp.int32)
    col_tile = (tile_index % COL_TILES).astype(jnp.int32)
    occupied = (slot_tile >= 0).astype(jnp.float32)
    shard_inputs = inputs.reshape(SHARDS, TOK_DEV, D)
    shard_grads = cotangent.reshape(SHARDS, TOK_DEV, KV)

    def one_shard(summed, shard_item):
        block_x, block_g, valid_count = shard_item
        valid_rows = (row_ids < valid_count)[:, None]
        masked = jnp.where(valid_rows, block_g, jnp.zeros_like(block_g))
        forward = jnp.dot(block_x, effective, preferred_element_type=jnp.float32)
        forward = jnp.where(valid_rows, forward, jnp.zeros_like(forward)).astype(jnp.bfloat16)
        backward = jnp.dot(masked, effective.T, preferred_element_type=jnp.float32).astype(jnp.bfloat16)
        x_tiles = jnp.take(block_x.reshape(TOK_DEV, ROW_TILES, BLOCK), row_tile, axis=1).astype(jnp.float32)
        g_tiles = jnp.take(masked.reshape(TOK_DEV, COL_TILES, BLOCK), col_tile, axis=1).astype(jnp.float32)
        summed = summed + jnp.einsum("tsa,tsb->sab", x_tiles, g_tiles)
        return summed, (forward, backward)

    start_sum = jnp.zeros((SLOTS, BLOCK, BLOCK), jnp.float32)
    summed, (forwards, backwards) = lax.scan(one_shard, start_sum, (shard_inputs, shard_grads, token_count))
    delta_grad = summed * occupied[:, None, None] / token_total
    return forwards.reshape(TOKENS, KV), backwards.reshape(TOKENS, D), delta_grad
```

```python
import functools

import jax
import jax.numpy as jnp
from jax import lax
from jax.experimental import pallas as pl
from jax.experimental.pallas import tpu as pltpu
from jax.sharding import PartitionSpec as P

NZ, NX, NC, NY = 8, 4, 2, 4
BF16, F32 = jnp.bfloat16, jnp.float32
EVEN = (2, 0, -2, 4)
FROM_UP = (3, 1)
FROM_DOWN = (-1, -3)


def fetch(v, dz=0, dx=0, dc=0):
    pairs = []
    for z in range(NZ):
        for x in range(NX):
            for c in range(NC):
                src = ((z + dz) % NZ * NX + (x + dx) % NX) * NC + (c ^ dc)
                pairs.append((src, (z * NX + x) * NC + c))
    return lax.ppermute(v, "fsdp", pairs)


def fetch_y(v, dy):
    return lax.ppermute(v, "dp", [((y + dy) % NY, y) for y in range(NY)])


def params(mib):
    return pltpu.CompilerParams(vmem_limit_bytes=mib * 2**20)


def grad_blocks(ids, pos, x_ref, m_ref, c_rel, emit):
    block = 128
    y, z, x, c = pos[0], pos[1], pos[2], pos[3]
    core = (c + c_rel) % 2

    def one(i, carry):
        xr, zr, k = i // (NZ * 2), (i // 2) % NZ, i % 2
        owner = ((z + zr) % NZ * NX + (x + xr) % NX) * NC + core
        tile = ids[owner * 2 + k]
        live = tile >= 0
        safe = jnp.maximum(tile, 0)
        row = zr * 64 + k * 32

        @pl.when(live)
        def _():
            xt = x_ref[:, pl.ds(pl.multiple_of(safe // 4 * block, block), block)]
            mt = m_ref[:, pl.ds(pl.multiple_of(safe % 4 * block, block), block)]
            part = lax.dot_general(xt, mt, (((0,), (0,)), ((), ())), preferred_element_type=F32)
            for q in range(NY):
                emit((q + NY - y) % NY, xr, pl.multiple_of(row, 32), part[q * 32 : q * 32 + 32])

        @pl.when(jnp.logical_not(live))
        def _():
            for q in range(NY):
                emit(q, xr, pl.multiple_of(row, 32), jnp.zeros((32, block), F32))

        return carry

    lax.fori_loop(0, NX * NZ * 2, one, 0, unroll=2)


def mask_rows(cot_ref, count, m_ref):
    rows = lax.broadcasted_iota(jnp.int32, cot_ref.shape, 0)
    g = cot_ref[...]
    m_ref[...] = jnp.where(rows < count, g, jnp.zeros_like(g))


def grads_away_kernel(ids, pos, x_ref, cot_ref, out_ref, m_ref):
    mask_rows(cot_ref, pos[4], m_ref)

    def emit(q, xr, row, v):
        out_ref[q, xr, pl.ds(row, 32), :] = v.astype(BF16)

    grad_blocks(ids, pos, x_ref, m_ref, 1, emit)


def grads_home_kernel(ids, pos, x_ref, cot_ref, r_ref, h0, h1, h2, h3, m_ref, t_ref):
    mask_rows(cot_ref, pos[4], m_ref)

    def emit(q, xr, row, v):
        t_ref[q, xr, pl.ds(row, 32), :] = v

    grad_blocks(ids, pos, x_ref, m_ref, 0, emit)
    for q, h in enumerate((h0, h1, h2, h3)):
        for xr in range(NX):
            h[xr] = (t_ref[q, xr] + r_ref[q, xr].astype(F32)).astype(h.dtype)


def vmem(n):
    return [pl.BlockSpec(memory_space=pltpu.VMEM)] * n


def smem(n):
    return [pl.BlockSpec(memory_space=pltpu.SMEM)] * n


def grads_away(ids, pos, x, cot):
    return pl.pallas_call(
        grads_away_kernel,
        out_shape=jax.ShapeDtypeStruct((NY, NX, 512, 128), BF16),
        in_specs=smem(2) + vmem(2),
        out_specs=vmem(1)[0],
        scratch_shapes=[pltpu.VMEM(cot.shape, BF16)],
        compiler_params=params(40),
        cost_estimate=pl.CostEstimate(flops=1_500_000_000, bytes_accessed=8_000_000, transcendentals=0),
        name="grads_away",
    )(ids, pos, x, cot)


def grads_home(ids, pos, x, cot, r):
    return pl.pallas_call(
        grads_home_kernel,
        out_shape=[jax.ShapeDtypeStruct((NX, 512, 128), d) for d in (F32, BF16, BF16, BF16)],
        in_specs=smem(2) + vmem(3),
        out_specs=vmem(4),
        scratch_shapes=[pltpu.VMEM(cot.shape, BF16), pltpu.VMEM((NY, NX, 512, 128), F32)],
        compiler_params=params(48),
        cost_estimate=pl.CostEstimate(flops=1_500_000_000, bytes_accessed=10_000_000, transcendentals=0),
        name="grads_home",
    )(ids, pos, x, cot, r)


def sum_y_kernel(a, b, c, d, j0, j1, j2, j3):
    for xr, j in enumerate((j0, j1, j2, j3)):
        s = a[xr] + b[xr].astype(F32) + c[xr].astype(F32) + d[xr].astype(F32)
        j[...] = s.astype(j.dtype)


def sum_y(*parts):
    return pl.pallas_call(
        sum_y_kernel,
        out_shape=[jax.ShapeDtypeStruct((512, 128), d) for d in (F32, BF16, BF16, BF16)],
        in_specs=vmem(4),
        out_specs=vmem(4),
        name="sum_y",
    )(*parts)


def sum_x_kernel(a, b, c, d, *outs):
    for zr, o in enumerate(outs):
        rows = slice(zr * 64, zr * 64 + 64)
        o[...] = a[rows, :] + b[rows, :].astype(F32) + c[rows, :].astype(F32) + d[rows, :].astype(F32)


def sum_x(*parts):
    return pl.pallas_call(
        sum_x_kernel,
        out_shape=[jax.ShapeDtypeStruct((64, 128), F32)] * NZ,
        in_specs=vmem(4),
        out_specs=vmem(NZ),
        name="sum_x",
    )(*parts)


def sum_z_kernel(ids, *refs):
    out = refs[-1]
    total = refs[0][...]
    for r in refs[1:-1]:
        total = total + r[...]
    out[0:64, :] = total
    out[64:72, :] = jnp.full((8, 128), ids[128].astype(F32), F32)


def sum_z(ids, *parts):
    return pl.pallas_call(
        sum_z_kernel,
        out_shape=jax.ShapeDtypeStruct((72, 128), F32),
        in_specs=smem(1) + vmem(NZ),
        out_specs=vmem(1)[0],
        name="sum_z",
    )(ids, *parts)


def finish_kernel(pos, v0, v1, v2, v3, out):
    y = pos[0]
    total = (v0[64:65, :] + v1[64:65, :]) + (v2[64:65, :] + v3[64:65, :])
    for j, v in enumerate((v0, v1, v2, v3)):
        q = (y + j) % NY
        for k in range(2):
            out[k, pl.ds(pl.multiple_of(q * 32, 32), 32), :] = v[k * 32 : k * 32 + 32, :] / total


def finish(pos, *parts):
    return pl.pallas_call(
        finish_kernel,
        out_shape=jax.ShapeDtypeStruct((2, 128, 128), F32),
        in_specs=smem(1) + vmem(4),
        out_specs=vmem(1)[0],
        name="finish",
    )(pos, *parts)


def products_kernel(chunk, ids, pos, x_ref, cot_ref, *refs):
    pieces, (proj_ref, grad_ref, w_ref, d_ref, m_ref, acc_ref, wsem, dsem) = refs[:20], refs[20:]
    step = pl.program_id(0)
    block = 128

    @pl.when(step == 0)
    def _():
        z, x, c = pos[1], pos[2], pos[3]
        copies = []

        def owner(dz, dx, dc):
            return ((z + dz + NZ) % NZ * NX + (x + dx) % NX) * NC + (c + dc) % 2

        def put_w(src, tile):
            rows = pl.ds(pl.multiple_of(tile * block, block), block)
            copies.append(pltpu.make_async_copy(src, w_ref.at[rows, :], wsem.at[len(copies)]))

        for dc in range(2):
            a, zp, zm = pieces[dc * 10 : dc * 10 + 4], pieces[dc * 10 + 4], pieces[dc * 10 + 5]
            for dx in range(NX):
                for i, dz in enumerate(EVEN):
                    put_w(a[dx].at[i], owner(dz, dx, dc))
                for i, dz in enumerate(FROM_UP):
                    put_w(zp.at[dx, i], owner(dz, dx, dc))
                for i, dz in enumerate(FROM_DOWN):
                    put_w(zm.at[dx, i], owner(dz, dx, dc))
        n = 0
        for dc in range(2):
            cs = pieces[dc * 10 + 6 : dc * 10 + 10]
            for dx in range(NX):
                for i, dz in enumerate(EVEN + FROM_UP + FROM_DOWN):
                    slots = pl.ds(owner(dz, dx, dc) * 2, 2)
                    copies.append(pltpu.make_async_copy(cs[dx].at[i], d_ref.at[slots], dsem.at[n]))
                    n += 1
        for copy in copies:
            copy.start()
        mask_rows(cot_ref, pos[4], m_ref)
        acc_ref[...] = jnp.zeros_like(acc_ref)
        for copy in copies:
            copy.wait()

        def add(s, carry):
            tile = ids[s]

            @pl.when(tile >= 0)
            def _():
                at = (
                    pl.ds(pl.multiple_of(tile // 4 * block, block), block),
                    pl.ds(pl.multiple_of(tile % 4 * block, block), block),
                )
                w_ref[at] = (w_ref[at].astype(F32) + d_ref[s].astype(F32)).astype(BF16)

            return carry

        lax.fori_loop(0, 128, add, 0)

    w = w_ref[pl.ds(pl.multiple_of(step * chunk, chunk), chunk), :]
    acc_ref[...] += jnp.dot(x_ref[...], w, preferred_element_type=F32)
    grad_ref[...] = lax.dot_general(
        m_ref[...], w, (((1,), (1,)), ((), ())), preferred_element_type=F32
    ).astype(BF16)

    @pl.when(step == pl.num_programs(0) - 1)
    def _():
        acc = acc_ref[...]
        rows = lax.broadcasted_iota(jnp.int32, acc.shape, 0)
        proj_ref[...] = jnp.where(rows < pos[4], acc, jnp.zeros_like(acc)).astype(BF16)


def products(ids, pos, x, cot, pieces):
    tokens, width = x.shape
    heads = cot.shape[1]
    chunk = 512
    return pl.pallas_call(
        functools.partial(products_kernel, chunk),
        grid=(width // chunk,),
        out_shape=[jax.ShapeDtypeStruct((tokens, heads), BF16), jax.ShapeDtypeStruct((tokens, width), BF16)],
        in_specs=smem(2)
        + [
            pl.BlockSpec((tokens, chunk), lambda i: (0, i)),
            pl.BlockSpec((tokens, heads), lambda i: (0, 0)),
        ]
        + [pl.BlockSpec(memory_space=pl.ANY)] * 20,
        out_specs=[
            pl.BlockSpec((tokens, heads), lambda i: (0, 0)),
            pl.BlockSpec((tokens, chunk), lambda i: (0, i)),
        ],
        scratch_shapes=[
            pltpu.VMEM((width, heads), BF16),
            pltpu.VMEM((128, 128, 128), BF16),
            pltpu.VMEM((tokens, heads), BF16),
            pltpu.VMEM((tokens, heads), F32),
            pltpu.SemaphoreType.DMA((64,)),
            pltpu.SemaphoreType.DMA((64,)),
        ],
        compiler_params=params(32),
        cost_estimate=pl.CostEstimate(flops=6_000_000_000, bytes_accessed=25_000_000, transcendentals=0),
        name="products",
    )(ids, pos, x, cot, *pieces)


def per_device(inputs, frozen, cotangent, delta_slots, slot_tile, token_count):
    f = lax.axis_index("fsdp")
    y = lax.axis_index("dp")
    here = jnp.zeros((256,), jnp.int32)
    here = lax.dynamic_update_slice(here, slot_tile, (2 * f,))
    here = lax.dynamic_update_slice(here, token_count, (128,))

    even = [fetch(frozen, dz=d) if d else frozen for d in EVEN]
    deven = [fetch(delta_slots, dz=d) if d else delta_slots for d in EVEN]
    ids = lax.psum(here, "fsdp")
    pos = jnp.stack([y, f // 8, f // 2 % 4, f % 2, token_count[0]]).astype(jnp.int32)

    away = grads_away(ids, pos, inputs, cotangent)
    back = fetch(away, dc=1)

    a0 = jnp.stack(even)
    a = [a0] + [fetch(a0, dx=d) for d in (1, 2, 3)]
    b0 = jnp.stack(deven)
    up, down = fetch(b0[0:2], dz=1), fetch(b0[1:3], dz=-1)

    h = grads_home(ids, pos, inputs, cotangent, back)
    got = [h[0], fetch_y(h[3], 1), fetch_y(h[2], 2), fetch_y(h[1], -1)]

    c0 = jnp.concatenate([b0, up, down])
    c = [c0] + [fetch(c0, dx=d) for d in (1, 2, 3)]
    zp = fetch(jnp.stack([v[0:2] for v in a]), dz=1)
    zm = fetch(jnp.stack([v[1:3] for v in a]), dz=-1)

    j = sum_y(*got)
    got = [j[0], fetch(j[3], dx=1), fetch(j[2], dx=2), fetch(j[1], dx=-1)]
    t = sum_x(*got)
    q = sum_z(ids, t[0], *[fetch(t[8 - d], dz=d) for d in range(1, 8)])
    owned = finish(pos, q, *[fetch_y(q, d) for d in (1, 2, 3)])

    mine = [*a, zp, zm, *c]
    pieces = mine + [fetch(v, dc=1) for v in mine]
    projected, grad_in = products(ids, pos, inputs, cotangent, pieces)
    return projected, grad_in, owned


def solution(mesh):
    in_specs = (
        P(("dp", "fsdp"), None),
        P("fsdp", None),
        P(("dp", "fsdp"), None),
        P("fsdp", None, None),
        P("fsdp"),
        P(("dp", "fsdp")),
    )
    out_specs = (P(("dp", "fsdp"), None), P(("dp", "fsdp"), None), P("fsdp", None, None))
    return jax.shard_map(per_device, mesh=mesh, in_specs=in_specs, out_specs=out_specs, check_vma=False)
```

```python
import functools

import jax
import jax.numpy as jnp
from jax import lax
from jax.experimental import pallas as pl
from jax.experimental.pallas import tpu as pltpu
from jax.sharding import PartitionSpec as P

NZ, NX, NC, NY = 8, 4, 2, 4
BF16, F32 = jnp.bfloat16, jnp.float32
OWNERS = NZ * NX


def fetch(v, offset):
    pairs = []
    for y in range(NY):
        for z in range(NZ):
            for x in range(NX):
                for c in range(NC):
                    dy, dz, dx, dc = offset(c)
                    near = (((y + dy) % NY * NZ + (z + dz) % NZ) * NX + (x + dx) % NX) * NC + (c ^ dc)
                    pairs.append((near, ((y * NZ + z) * NX + x) * NC + c))
    return lax.ppermute(v, ("dp", "fsdp"), pairs)


def exchange(sent, offset):
    n = len(sent)
    signed = lambda j: j - n if j > n // 2 else j
    return [fetch(sent[n - j], lambda c, j=j: offset(c, signed(j))) for j in range(1, n)]


def other_core(v):
    return fetch(v, lambda c: (0, 0, 0, 1))


def y_or_x(c, d):
    return (d, 0, 0, 0) if c == 0 else (0, 0, d, 0)


def x_or_y(c, d):
    return y_or_x(1 - c, d)


def along_z(c, d):
    return (0, d, 0, 0)


def params(mib):
    return pltpu.CompilerParams(vmem_limit_bytes=mib * 2**20)


def vmem(n):
    return [pl.BlockSpec(memory_space=pltpu.VMEM)] * n


def smem(n):
    return [pl.BlockSpec(memory_space=pltpu.SMEM)] * n


def grad_blocks(ids, core, x_ref, mt_ref, emit):
    block = 128

    def one(i, carry):
        tile = ids[((i // 2 % NZ * NX + i // (2 * NZ)) * NC + core) * 2 + i % 2]
        safe = jnp.maximum(tile, 0)
        xt = x_ref[:, pl.ds(pl.multiple_of(safe // 4 * block, block), block)]
        mt = mt_ref[pl.ds(pl.multiple_of(safe % 4 * block, block), block), :]
        part = jnp.dot(mt, xt, preferred_element_type=F32)
        emit(i, jnp.where(tile >= 0, part, jnp.zeros_like(part)))
        return carry

    lax.fori_loop(0, OWNERS * 2, one, 0, unroll=4)


def grads_away_kernel(ids, pos, x_ref, cot_ref, out_ref, mt_ref):
    rows = lax.broadcasted_iota(jnp.int32, cot_ref.shape, 0)
    g = cot_ref[...]
    mt_ref[...] = jnp.where(rows < pos[4], g, jnp.zeros_like(g)).T

    def emit(i, v):
        out_ref[i] = v.astype(BF16)

    grad_blocks(ids, 1 - pos[3], x_ref, mt_ref, emit)


def grads_home_kernel(ids, pos, x_ref, mt_ref, r_ref, h0, h1, h2, h3, t_ref):
    def emit(i, v):
        t_ref[i] = v + r_ref[i].astype(F32)

    grad_blocks(ids, pos[3], x_ref, mt_ref, emit)
    @pl.when(pos[3] == 0)
    def _():
        for j, h in enumerate((h0, h1, h2, h3)):
            q = (pos[0] + j) % NY
            h[...] = t_ref[:, pl.ds(pl.multiple_of(q * 32, 32), 32), :].astype(h.dtype)

    @pl.when(pos[3] == 1)
    def _():
        for j, h in enumerate((h0, h1, h2, h3)):
            x = (pos[2] + j) % NX
            h[...] = t_ref[pl.ds(x * 16, 16)].reshape(OWNERS * 2, 32, 128).astype(h.dtype)


def grads_away(ids, pos, x, cot):
    return pl.pallas_call(
        grads_away_kernel,
        out_shape=[
            jax.ShapeDtypeStruct((OWNERS * 2, 128, 128), BF16),
            jax.ShapeDtypeStruct(cot.shape[::-1], BF16),
        ],
        in_specs=smem(2) + vmem(2),
        out_specs=vmem(2),
        compiler_params=params(32),
        cost_estimate=pl.CostEstimate(flops=3_000_000_000, bytes_accessed=8_000_000, transcendentals=0),
        name="grads_away",
    )(ids, pos, x, cot)


def grads_home(ids, pos, x, mt, r):
    return pl.pallas_call(
        grads_home_kernel,
        out_shape=[jax.ShapeDtypeStruct((OWNERS * 2, 32, 128), d) for d in (F32, BF16, BF16, BF16)],
        in_specs=smem(2) + vmem(3),
        out_specs=vmem(4),
        scratch_shapes=[pltpu.VMEM((OWNERS * 2, 128, 128), F32)],
        compiler_params=params(32),
        cost_estimate=pl.CostEstimate(flops=3_000_000_000, bytes_accessed=10_000_000, transcendentals=0),
        name="grads_home",
    )(ids, pos, x, mt, r)


def sum_first_kernel(pos, a, b, c, d, j0, j1, j2, j3, t_ref):
    t_ref[...] = a[...] + b[...].astype(F32) + c[...].astype(F32) + d[...].astype(F32)

    @pl.when(pos[3] == 0)
    def _():
        for j, o in enumerate((j0, j1, j2, j3)):
            x = (pos[2] + j) % NX
            o[...] = t_ref[pl.ds(x * 16, 16)].astype(o.dtype)

    @pl.when(pos[3] == 1)
    def _():
        for j, o in enumerate((j0, j1, j2, j3)):
            q = (pos[0] + j) % NY
            for i in range(16):
                o[i] = t_ref[i * 4 + q].astype(o.dtype)


def sum_first(pos, *parts):
    return pl.pallas_call(
        sum_first_kernel,
        out_shape=[jax.ShapeDtypeStruct((16, 32, 128), d) for d in (F32, BF16, BF16, BF16)],
        in_specs=smem(1) + vmem(4),
        out_specs=vmem(4),
        scratch_shapes=[pltpu.VMEM(parts[0].shape, F32)],
        compiler_params=params(16),
        name="sum_first",
    )(pos, *parts)


def sum_second_kernel(pos, a, b, c, d, *refs):
    outs, t_ref = refs[:-1], refs[-1]
    t_ref[...] = a[...] + b[...].astype(F32) + c[...].astype(F32) + d[...].astype(F32)
    for j, o in enumerate(outs):
        z = (pos[1] + j) % NZ
        o[...] = t_ref[pl.ds(z * 2, 2)]


def sum_second(pos, *parts):
    return pl.pallas_call(
        sum_second_kernel,
        out_shape=[jax.ShapeDtypeStruct((2, 32, 128), F32)] * NZ,
        in_specs=smem(1) + vmem(4),
        out_specs=vmem(NZ),
        scratch_shapes=[pltpu.VMEM(parts[0].shape, F32)],
        compiler_params=params(16),
        name="sum_second",
    )(pos, *parts)


def sum_third_kernel(ids, *refs):
    out = refs[-1]
    total = refs[0][...]
    for r in refs[1:-1]:
        total = total + r[...]
    out[0:64, :] = total.reshape(64, 128)
    out[64:72, :] = jnp.full((8, 128), ids[128].astype(F32), F32)


def sum_third(ids, *parts):
    return pl.pallas_call(
        sum_third_kernel,
        out_shape=jax.ShapeDtypeStruct((72, 128), F32),
        in_specs=smem(1) + vmem(NZ),
        out_specs=vmem(1)[0],
        name="sum_third",
    )(ids, *parts)


def finish_kernel(pos, v0, v1, v2, v3, out, t_ref):
    total = (v0[64:65, :] + v1[64:65, :]) + (v2[64:65, :] + v3[64:65, :])
    for j, v in enumerate((v0, v1, v2, v3)):
        q = (pos[0] + j) % NY
        for k in range(2):
            t_ref[k, pl.ds(pl.multiple_of(q * 32, 32), 32), :] = v[k * 32 : k * 32 + 32, :] / total
    for k in range(2):
        out[k] = t_ref[k].T


def finish(pos, *parts):
    return pl.pallas_call(
        finish_kernel,
        out_shape=jax.ShapeDtypeStruct((2, 128, 128), F32),
        in_specs=smem(1) + vmem(4),
        out_specs=vmem(1)[0],
        scratch_shapes=[pltpu.VMEM((2, 128, 128), F32)],
        name="finish",
    )(pos, *parts)


def pack_kernel(frozen_ref, delta_ref, out):
    out[0:128, :] = frozen_ref[...]
    for k in range(2):
        for half in range(2):
            col = (2 * k + half) * 128
            out[128:192, col : col + 128] = delta_ref[k, half * 64 : half * 64 + 64, :]


def pack(frozen, delta_slots):
    return pl.pallas_call(
        pack_kernel,
        out_shape=jax.ShapeDtypeStruct((192, 512), BF16),
        in_specs=vmem(2),
        out_specs=vmem(1)[0],
        name="pack",
    )(frozen, delta_slots)


TILES_A_STEP = 4


def products_kernel(inverse, pos, x_ref, cot_ref, w_ref, all_ref, proj_ref, grad_ref, d_ref, m_ref, acc_ref, e_ref, sem):
    step = pl.program_id(0)
    block = 128
    rows = lax.broadcasted_iota(jnp.int32, acc_ref.shape, 0)

    @pl.when(step == 0)
    def _():
        copy = pltpu.make_async_copy(all_ref.at[:, 128:192, :], d_ref, sem)
        copy.start()
        g = cot_ref[...]
        m_ref[...] = jnp.where(rows < pos[4], g, jnp.zeros_like(g))
        acc_ref[...] = jnp.zeros_like(acc_ref)
        copy.wait()

    for j in range(TILES_A_STEP):
        for col in range(4):
            slot = inverse[(step * TILES_A_STEP + j) * 4 + col]
            safe = jnp.maximum(slot, 0)
            for half in range(2):
                lanes = pl.ds(pl.multiple_of((safe % 2 * 2 + half) * block, block), block)
                d = d_ref[safe // 2, :, lanes].astype(F32)
                d = jnp.where(slot >= 0, d, jnp.zeros_like(d))
                at = slice(half * 64, half * 64 + 64), slice(col * block, col * block + block)
                w = w_ref[j, at[0], at[1]].astype(F32)
                e_ref[j * block + half * 64 : j * block + half * 64 + 64, at[1]] = (w + d).astype(BF16)

    w = e_ref[...]
    acc_ref[...] += jnp.dot(x_ref[...], w, preferred_element_type=F32)
    grad_ref[...] = lax.dot_general(
        m_ref[...], w, (((1,), (1,)), ((), ())), preferred_element_type=F32
    ).astype(BF16)

    @pl.when(step == pl.num_programs(0) - 1)
    def _():
        acc = acc_ref[...]
        proj_ref[...] = jnp.where(rows < pos[4], acc, jnp.zeros_like(acc)).astype(BF16)


def products(inverse, pos, x, cot, gathered):
    tokens, width = x.shape
    heads = cot.shape[1]
    chunk = TILES_A_STEP * 128
    return pl.pallas_call(
        products_kernel,
        grid=(width // chunk,),
        out_shape=[jax.ShapeDtypeStruct((tokens, heads), BF16), jax.ShapeDtypeStruct((tokens, width), BF16)],
        in_specs=smem(2)
        + [
            pl.BlockSpec((tokens, chunk), lambda i: (0, i)),
            pl.BlockSpec((tokens, heads), lambda i: (0, 0)),
            pl.BlockSpec((TILES_A_STEP, 128, heads), lambda i: (i, 0, 0)),
            pl.BlockSpec(memory_space=pl.ANY),
        ],
        out_specs=[
            pl.BlockSpec((tokens, heads), lambda i: (0, 0)),
            pl.BlockSpec((tokens, chunk), lambda i: (0, i)),
        ],
        scratch_shapes=[
            pltpu.VMEM((64, 64, heads), BF16),
            pltpu.VMEM((tokens, heads), BF16),
            pltpu.VMEM((tokens, heads), F32),
            pltpu.VMEM((chunk, heads), BF16),
            pltpu.SemaphoreType.DMA,
        ],
        compiler_params=params(60),
        cost_estimate=pl.CostEstimate(flops=6_000_000_000, bytes_accessed=25_000_000, transcendentals=0),
        name="products",
    )(inverse, pos, x, cot, gathered, gathered)


def per_device(inputs, frozen, cotangent, delta_slots, slot_tile, token_count):
    f = lax.axis_index("fsdp")
    y = lax.axis_index("dp")
    gathered = lax.all_gather(pack(frozen, delta_slots), "fsdp", axis=0)
    here = jnp.zeros((256,), jnp.int32)
    here = lax.dynamic_update_slice(here, slot_tile, (2 * f,))
    here = lax.dynamic_update_slice(here, token_count, (128,))
    ids = lax.psum(here, "fsdp")
    pos = jnp.stack([y, f // 8, f // 2 % 4, f % 2, token_count[0]]).astype(jnp.int32)

    away, mt = grads_away(ids, pos, inputs, cotangent)
    h = grads_home(ids, pos, inputs, mt, other_core(away))
    j = sum_first(pos, h[0], *exchange(h, y_or_x))
    t = sum_second(pos, j[0], *exchange(j, x_or_y))
    q = sum_third(ids, t[0], *exchange(t, along_z))
    owned = finish(pos, q, *[fetch(q, lambda c, d=d: (d, 0, 0, 0)) for d in (1, 2, 3)])

    slots = jnp.arange(128, dtype=jnp.int32)
    tiles = jnp.arange(256, dtype=jnp.int32)
    inverse = jnp.max(jnp.where(ids[None, :128] == tiles[:, None], slots[None, :], -1), axis=1)
    projected, grad_in = products(inverse, pos, inputs, cotangent, gathered)
    return projected, grad_in, owned


def solution(mesh):
    in_specs = (
        P(("dp", "fsdp"), None),
        P("fsdp", None),
        P(("dp", "fsdp"), None),
        P("fsdp", None, None),
        P("fsdp"),
        P(("dp", "fsdp")),
    )
    out_specs = (P(("dp", "fsdp"), None), P(("dp", "fsdp"), None), P("fsdp", None, None))
    return jax.shard_map(per_device, mesh=mesh, in_specs=in_specs, out_specs=out_specs, check_vma=False)
```

```python
import functools

import jax
import jax.numpy as jnp
from jax import lax
from jax.experimental import pallas as pl
from jax.experimental.pallas import tpu as pltpu
from jax.sharding import PartitionSpec as P

NZ, NX, NC, NY = 8, 4, 2, 4
BF16, F32 = jnp.bfloat16, jnp.float32
OWNERS = NZ * NX


def fetch(v, offset):
    pairs = []
    for y in range(NY):
        for z in range(NZ):
            for x in range(NX):
                for c in range(NC):
                    dy, dz, dx, dc = offset(c)
                    near = (((y + dy) % NY * NZ + (z + dz) % NZ) * NX + (x + dx) % NX) * NC + (c ^ dc)
                    pairs.append((near, ((y * NZ + z) * NX + x) * NC + c))
    return lax.ppermute(v, ("dp", "fsdp"), pairs)


def exchange(sent, offset):
    n = len(sent)
    signed = lambda j: j - n if j > n // 2 else j
    return [fetch(sent[n - j], lambda c, j=j: offset(c, signed(j))) for j in range(1, n)]


def other_core(v):
    return fetch(v, lambda c: (0, 0, 0, 1))


def y_or_x(c, d):
    return (d, 0, 0, 0) if c == 0 else (0, 0, d, 0)


def x_or_y(c, d):
    return y_or_x(1 - c, d)


def along_z(c, d):
    return (0, d, 0, 0)


def params(mib):
    return pltpu.CompilerParams(vmem_limit_bytes=mib * 2**20)


def vmem(n):
    return [pl.BlockSpec(memory_space=pltpu.VMEM)] * n


def smem(n):
    return [pl.BlockSpec(memory_space=pltpu.SMEM)] * n


def grad_blocks(ids, core, x_ref, mt_ref, emit):
    block = 128

    def one(i, carry):
        tile = ids[((i // 2 % NZ * NX + i // (2 * NZ)) * NC + core) * 2 + i % 2]
        safe = jnp.maximum(tile, 0)
        xt = x_ref[:, pl.ds(pl.multiple_of(safe // 4 * block, block), block)]
        mt = mt_ref[pl.ds(pl.multiple_of(safe % 4 * block, block), block), :]
        part = jnp.dot(mt, xt, preferred_element_type=F32)
        emit(i, jnp.where(tile >= 0, part, jnp.zeros_like(part)))
        return carry

    lax.fori_loop(0, OWNERS * 2, one, 0, unroll=4)


def grads_away_kernel(ids, pos, x_ref, cot_ref, out_ref, mt_ref):
    rows = lax.broadcasted_iota(jnp.int32, cot_ref.shape, 0)
    g = cot_ref[...]
    mt_ref[...] = jnp.where(rows < pos[4], g, jnp.zeros_like(g)).T

    def emit(i, v):
        out_ref[i] = v.astype(BF16)

    grad_blocks(ids, 1 - pos[3], x_ref, mt_ref, emit)


def grads_home_kernel(ids, pos, x_ref, mt_ref, r_ref, h0, h1, h2, h3, t_ref):
    def emit(i, v):
        t_ref[i] = v + r_ref[i].astype(F32)

    grad_blocks(ids, pos[3], x_ref, mt_ref, emit)
    @pl.when(pos[3] == 0)
    def _():
        for j, h in enumerate((h0, h1, h2, h3)):
            q = (pos[0] + j) % NY
            h[...] = t_ref[:, pl.ds(pl.multiple_of(q * 32, 32), 32), :].astype(h.dtype)

    @pl.when(pos[3] == 1)
    def _():
        for j, h in enumerate((h0, h1, h2, h3)):
            x = (pos[2] + j) % NX
            h[...] = t_ref[pl.ds(x * 16, 16)].reshape(OWNERS * 2, 32, 128).astype(h.dtype)


def grads_away(ids, pos, x, cot):
    return pl.pallas_call(
        grads_away_kernel,
        out_shape=[
            jax.ShapeDtypeStruct((OWNERS * 2, 128, 128), BF16),
            jax.ShapeDtypeStruct(cot.shape[::-1], BF16),
        ],
        in_specs=smem(2) + vmem(2),
        out_specs=vmem(2),
        compiler_params=params(32),
        cost_estimate=pl.CostEstimate(flops=3_000_000_000, bytes_accessed=8_000_000, transcendentals=0),
        name="grads_away",
    )(ids, pos, x, cot)


def grads_home(ids, pos, x, mt, r):
    return pl.pallas_call(
        grads_home_kernel,
        out_shape=[jax.ShapeDtypeStruct((OWNERS * 2, 32, 128), d) for d in (F32, BF16, BF16, BF16)],
        in_specs=smem(2) + vmem(3),
        out_specs=vmem(4),
        scratch_shapes=[pltpu.VMEM((OWNERS * 2, 128, 128), F32)],
        compiler_params=params(32),
        cost_estimate=pl.CostEstimate(flops=3_000_000_000, bytes_accessed=10_000_000, transcendentals=0),
        name="grads_home",
    )(ids, pos, x, mt, r)


def sum_first_kernel(pos, a, b, c, d, j0, j1, j2, j3, t_ref):
    t_ref[...] = a[...] + b[...].astype(F32) + c[...].astype(F32) + d[...].astype(F32)

    @pl.when(pos[3] == 0)
    def _():
        for j, o in enumerate((j0, j1, j2, j3)):
            x = (pos[2] + j) % NX
            o[...] = t_ref[pl.ds(x * 16, 16)].astype(o.dtype)

    @pl.when(pos[3] == 1)
    def _():
        for j, o in enumerate((j0, j1, j2, j3)):
            q = (pos[0] + j) % NY
            for i in range(16):
                o[i] = t_ref[i * 4 + q].astype(o.dtype)


def sum_first(pos, *parts):
    return pl.pallas_call(
        sum_first_kernel,
        out_shape=[jax.ShapeDtypeStruct((16, 32, 128), d) for d in (F32, BF16, BF16, BF16)],
        in_specs=smem(1) + vmem(4),
        out_specs=vmem(4),
        scratch_shapes=[pltpu.VMEM(parts[0].shape, F32)],
        compiler_params=params(16),
        name="sum_first",
    )(pos, *parts)


def sum_second_kernel(pos, a, b, c, d, *refs):
    outs, t_ref = refs[:-1], refs[-1]
    t_ref[...] = a[...] + b[...].astype(F32) + c[...].astype(F32) + d[...].astype(F32)
    for j, o in enumerate(outs):
        z = (pos[1] + j) % NZ
        o[...] = t_ref[pl.ds(z * 2, 2)]


def sum_second(pos, *parts):
    return pl.pallas_call(
        sum_second_kernel,
        out_shape=[jax.ShapeDtypeStruct((2, 32, 128), F32)] * NZ,
        in_specs=smem(1) + vmem(4),
        out_specs=vmem(NZ),
        scratch_shapes=[pltpu.VMEM(parts[0].shape, F32)],
        compiler_params=params(16),
        name="sum_second",
    )(pos, *parts)


def sum_third_kernel(ids, *refs):
    out = refs[-1]
    total = refs[0][...]
    for r in refs[1:-1]:
        total = total + r[...]
    out[0:64, :] = total.reshape(64, 128)
    out[64:72, :] = jnp.full((8, 128), ids[128].astype(F32), F32)


def sum_third(ids, *parts):
    return pl.pallas_call(
        sum_third_kernel,
        out_shape=jax.ShapeDtypeStruct((72, 128), F32),
        in_specs=smem(1) + vmem(NZ),
        out_specs=vmem(1)[0],
        name="sum_third",
    )(ids, *parts)


def finish_kernel(pos, v0, v1, v2, v3, after, out, t_ref):
    total = (v0[64:65, :] + v1[64:65, :]) + (v2[64:65, :] + v3[64:65, :])
    for j, v in enumerate((v0, v1, v2, v3)):
        q = (pos[0] + j) % NY
        for k in range(2):
            t_ref[k, pl.ds(pl.multiple_of(q * 32, 32), 32), :] = v[k * 32 : k * 32 + 32, :] / total
    for k in range(2):
        out[k] = t_ref[k].T


def finish(pos, parts, after):
    return pl.pallas_call(
        finish_kernel,
        out_shape=jax.ShapeDtypeStruct((2, 128, 128), F32),
        in_specs=smem(1) + vmem(4) + [pl.BlockSpec(memory_space=pl.ANY)],
        out_specs=vmem(1)[0],
        scratch_shapes=[pltpu.VMEM((2, 128, 128), F32)],
        name="finish",
    )(pos, *parts, after)


def pack_kernel(frozen_ref, delta_ref, out):
    out[0:128, :] = frozen_ref[...]
    for k in range(2):
        for half in range(2):
            col = (2 * k + half) * 128
            out[128:192, col : col + 128] = delta_ref[k, half * 64 : half * 64 + 64, :]


def pack(frozen, delta_slots):
    return pl.pallas_call(
        pack_kernel,
        out_shape=jax.ShapeDtypeStruct((192, 512), BF16),
        in_specs=vmem(2),
        out_specs=vmem(1)[0],
        name="pack",
    )(frozen, delta_slots)


CHUNK = 8


def build(inverse, w_ref, d_ref, e_ref, chunk):
    for j in range(CHUNK):
        tile = chunk * CHUNK + j
        for col in range(4):
            slot = inverse[tile * 4 + col]
            safe = jnp.maximum(slot, 0)
            lanes = slice(col * 128, col * 128 + 128)
            for half in range(2):
                at = pl.ds(pl.multiple_of((safe % 2 * 2 + half) * 128, 128), 128)
                d = d_ref[safe // 2, :, at].astype(F32)
                d = jnp.where(slot >= 0, d, jnp.zeros_like(d))
                rows = slice(half * 64, half * 64 + 64)
                e_ref[j, rows, lanes] = (w_ref[tile, rows, lanes].astype(F32) + d).astype(BF16)


def products_kernel(inverse, pos, x_ref, cot_ref, all_ref, proj_ref, grad_ref, w_ref, d_ref, m_ref, acc_ref, e0, e1, wsem, dsem):
    step, steps = pl.program_id(0), pl.num_programs(0)
    width = CHUNK * 128
    rows = lax.broadcasted_iota(jnp.int32, acc_ref.shape, 0)

    def weights(n):
        tiles = pl.ds(n * 2 * CHUNK, 2 * CHUNK)
        return pltpu.make_async_copy(all_ref.at[tiles, 0:128, :], w_ref.at[tiles], wsem.at[n])

    @pl.when(step == 0)
    def _():
        deltas = pltpu.make_async_copy(all_ref.at[:, 128:192, :], d_ref, dsem)
        deltas.start()
        weights(0).start()
        g = cot_ref[...]
        m_ref[...] = jnp.where(rows < pos[4], g, jnp.zeros_like(g))
        acc_ref[...] = jnp.zeros_like(acc_ref)
        deltas.wait()
        weights(1).start()
        weights(2).start()
        weights(0).wait()
        build(inverse, w_ref, d_ref, e0, 0)

    def multiply(e_ref, part):
        w = e_ref[...].reshape(width, acc_ref.shape[1])
        lanes = slice(part * width, part * width + width)
        acc_ref[...] += jnp.dot(x_ref[:, lanes], w, preferred_element_type=F32)
        grad_ref[:, lanes] = lax.dot_general(
            m_ref[...], w, (((1,), (1,)), ((), ())), preferred_element_type=F32
        ).astype(BF16)

    build(inverse, w_ref, d_ref, e1, step * 2 + 1)
    multiply(e0, 0)

    @pl.when(step < steps - 1)
    def _():
        @pl.when(step < steps - 3)
        def _():
            weights(step + 3).start()

        weights(step + 1).wait()

    build(inverse, w_ref, d_ref, e0, jnp.minimum(step * 2 + 2, 2 * steps - 1))
    multiply(e1, 1)

    @pl.when(step == steps - 1)
    def _():
        acc = acc_ref[...]
        proj_ref[...] = jnp.where(rows < pos[4], acc, jnp.zeros_like(acc)).astype(BF16)


def products(inverse, pos, x, cot, gathered):
    tokens, width = x.shape
    heads = cot.shape[1]
    wide = 2 * CHUNK * 128
    return pl.pallas_call(
        products_kernel,
        grid=(width // wide,),
        out_shape=[jax.ShapeDtypeStruct((tokens, heads), BF16), jax.ShapeDtypeStruct((tokens, width), BF16)],
        in_specs=smem(2)
        + [
            pl.BlockSpec((tokens, wide), lambda i: (0, i)),
            pl.BlockSpec((tokens, heads), lambda i: (0, 0)),
            pl.BlockSpec(memory_space=pl.ANY),
        ],
        out_specs=[
            pl.BlockSpec((tokens, heads), lambda i: (0, 0)),
            pl.BlockSpec((tokens, wide), lambda i: (0, i)),
        ],
        scratch_shapes=[
            pltpu.VMEM((64, 128, heads), BF16),
            pltpu.VMEM((64, 64, heads), BF16),
            pltpu.VMEM((tokens, heads), BF16),
            pltpu.VMEM((tokens, heads), F32),
            pltpu.VMEM((CHUNK, 128, heads), BF16),
            pltpu.VMEM((CHUNK, 128, heads), BF16),
            pltpu.SemaphoreType.DMA((64 // (2 * CHUNK),)),
            pltpu.SemaphoreType.DMA,
        ],
        compiler_params=params(60),
        cost_estimate=pl.CostEstimate(flops=6_000_000_000, bytes_accessed=25_000_000, transcendentals=0),
        name="products",
    )(inverse, pos, x, cot, gathered)


def per_device(inputs, frozen, cotangent, delta_slots, slot_tile, token_count):
    f = lax.axis_index("fsdp")
    y = lax.axis_index("dp")
    gathered = lax.all_gather(pack(frozen, delta_slots), "fsdp", axis=0)
    here = jnp.zeros((256,), jnp.int32)
    here = lax.dynamic_update_slice(here, slot_tile, (2 * f,))
    here = lax.dynamic_update_slice(here, token_count, (128,))
    ids = lax.psum(here, "fsdp")
    pos = jnp.stack([y, f // 8, f // 2 % 4, f % 2, token_count[0]]).astype(jnp.int32)

    away, mt = grads_away(ids, pos, inputs, cotangent)
    h = grads_home(ids, pos, inputs, mt, other_core(away))
    j = sum_first(pos, h[0], *exchange(h, y_or_x))
    t = sum_second(pos, j[0], *exchange(j, x_or_y))
    q = sum_third(ids, t[0], *exchange(t, along_z))
    last = [fetch(q, lambda c, d=d: (d, 0, 0, 0)) for d in (1, 2, 3)]

    slots = jnp.arange(128, dtype=jnp.int32)
    tiles = jnp.arange(256, dtype=jnp.int32)
    inverse = jnp.max(jnp.where(ids[None, :128] == tiles[:, None], slots[None, :], -1), axis=1)
    projected, grad_in = products(inverse, pos, inputs, cotangent, gathered)
    owned = finish(pos, [q, *last], projected)
    return projected, grad_in, owned


def solution(mesh):
    in_specs = (
        P(("dp", "fsdp"), None),
        P("fsdp", None),
        P(("dp", "fsdp"), None),
        P("fsdp", None, None),
        P("fsdp"),
        P(("dp", "fsdp")),
    )
    out_specs = (P(("dp", "fsdp"), None), P(("dp", "fsdp"), None), P("fsdp", None, None))
    return jax.shard_map(per_device, mesh=mesh, in_specs=in_specs, out_specs=out_specs, check_vma=False)
```

```python
import functools

import jax
import jax.numpy as jnp
from jax import lax
from jax.experimental import pallas as pl
from jax.experimental.pallas import tpu as pltpu
from jax.sharding import PartitionSpec as P

NZ, NX, NC, NY = 8, 4, 2, 4
BF16, F32 = jnp.bfloat16, jnp.float32
OWNERS = NZ * NX


def fetch(v, offset):
    pairs = []
    for y in range(NY):
        for z in range(NZ):
            for x in range(NX):
                for c in range(NC):
                    dy, dz, dx, dc = offset(c)
                    near = (((y + dy) % NY * NZ + (z + dz) % NZ) * NX + (x + dx) % NX) * NC + (c ^ dc)
                    pairs.append((near, ((y * NZ + z) * NX + x) * NC + c))
    return lax.ppermute(v, ("dp", "fsdp"), pairs)


def exchange(sent, offset):
    n = len(sent)
    signed = lambda j: j - n if j > n // 2 else j
    return [fetch(sent[n - j], lambda c, j=j: offset(c, signed(j))) for j in range(1, n)]


def other_core(v):
    return fetch(v, lambda c: (0, 0, 0, 1))


def y_or_x(c, d):
    return (d, 0, 0, 0) if c == 0 else (0, 0, d, 0)


def x_or_y(c, d):
    return y_or_x(1 - c, d)


def along_z(c, d):
    return (0, d, 0, 0)


def params(mib):
    return pltpu.CompilerParams(vmem_limit_bytes=mib * 2**20)


def vmem(n):
    return [pl.BlockSpec(memory_space=pltpu.VMEM)] * n


def smem(n):
    return [pl.BlockSpec(memory_space=pltpu.SMEM)] * n


def grad_blocks(ids, core, x_ref, mt_ref, live_ref, emit):
    block, unroll = 128, 4

    def tile_of(i):
        return ids[((i // 2 % NZ * NX + i // (2 * NZ)) * NC + core) * 2 + i % 2]

    def note(i, n):
        live_ref[n] = i
        return n + (tile_of(i) >= 0).astype(jnp.int32)

    n = lax.fori_loop(0, OWNERS * 2, note, 0, unroll=8)
    for p in range(unroll):
        live_ref[n + p] = live_ref[0]

    def one(r, carry):
        for p in range(unroll):
            i = live_ref[r * unroll + p]
            tile = tile_of(i)
            xt = x_ref[:, pl.ds(pl.multiple_of(tile // 4 * block, block), block)]
            mt = mt_ref[pl.ds(pl.multiple_of(tile % 4 * block, block), block), :]
            emit(i, jnp.dot(mt, xt, preferred_element_type=F32))
        return carry

    lax.fori_loop(0, (n + unroll - 1) // unroll, one, 0)


def grads_away_kernel(ids, pos, x_ref, cot_ref, out_ref, mt_ref, live_ref):
    rows = lax.broadcasted_iota(jnp.int32, cot_ref.shape, 0)
    g = cot_ref[...]
    mt_ref[...] = jnp.where(rows < pos[4], g, jnp.zeros_like(g)).T
    out_ref[...] = jnp.zeros_like(out_ref)

    def emit(i, v):
        out_ref[i] = v.astype(BF16)

    grad_blocks(ids, 1 - pos[3], x_ref, mt_ref, live_ref, emit)


def grads_home_kernel(ids, pos, x_ref, mt_ref, r_ref, h0, h1, h2, h3, t_ref, live_ref):
    t_ref[...] = r_ref[...].astype(F32)

    def emit(i, v):
        t_ref[i] = v + r_ref[i].astype(F32)

    grad_blocks(ids, pos[3], x_ref, mt_ref, live_ref, emit)
    @pl.when(pos[3] == 0)
    def _():
        for j, h in enumerate((h0, h1, h2, h3)):
            q = (pos[0] + j) % NY
            h[...] = t_ref[:, pl.ds(pl.multiple_of(q * 32, 32), 32), :].astype(h.dtype)

    @pl.when(pos[3] == 1)
    def _():
        for j, h in enumerate((h0, h1, h2, h3)):
            x = (pos[2] + j) % NX
            h[...] = t_ref[pl.ds(x * 16, 16)].reshape(OWNERS * 2, 32, 128).astype(h.dtype)


def grads_away(ids, pos, x, cot):
    return pl.pallas_call(
        grads_away_kernel,
        out_shape=[
            jax.ShapeDtypeStruct((OWNERS * 2, 128, 128), BF16),
            jax.ShapeDtypeStruct(cot.shape[::-1], BF16),
        ],
        in_specs=smem(2) + vmem(2),
        out_specs=vmem(2),
        scratch_shapes=[pltpu.SMEM((OWNERS * 2 + 8,), jnp.int32)],
        compiler_params=params(32),
        cost_estimate=pl.CostEstimate(flops=3_000_000_000, bytes_accessed=8_000_000, transcendentals=0),
        name="grads_away",
    )(ids, pos, x, cot)


def grads_home(ids, pos, x, mt, r):
    return pl.pallas_call(
        grads_home_kernel,
        out_shape=[jax.ShapeDtypeStruct((OWNERS * 2, 32, 128), d) for d in (F32, BF16, BF16, BF16)],
        in_specs=smem(2) + vmem(3),
        out_specs=vmem(4),
        scratch_shapes=[pltpu.VMEM((OWNERS * 2, 128, 128), F32), pltpu.SMEM((OWNERS * 2 + 8,), jnp.int32)],
        compiler_params=params(32),
        cost_estimate=pl.CostEstimate(flops=3_000_000_000, bytes_accessed=10_000_000, transcendentals=0),
        name="grads_home",
    )(ids, pos, x, mt, r)


def sum_first_kernel(pos, a, b, c, d, j0, j1, j2, j3, t_ref):
    t_ref[...] = a[...] + b[...].astype(F32) + c[...].astype(F32) + d[...].astype(F32)

    @pl.when(pos[3] == 0)
    def _():
        for j, o in enumerate((j0, j1, j2, j3)):
            x = (pos[2] + j) % NX
            o[...] = t_ref[pl.ds(x * 16, 16)].astype(o.dtype)

    @pl.when(pos[3] == 1)
    def _():
        for j, o in enumerate((j0, j1, j2, j3)):
            q = (pos[0] + j) % NY
            for i in range(16):
                o[i] = t_ref[i * 4 + q].astype(o.dtype)


def sum_first(pos, *parts):
    return pl.pallas_call(
        sum_first_kernel,
        out_shape=[jax.ShapeDtypeStruct((16, 32, 128), d) for d in (F32, BF16, BF16, BF16)],
        in_specs=smem(1) + vmem(4),
        out_specs=vmem(4),
        scratch_shapes=[pltpu.VMEM(parts[0].shape, F32)],
        compiler_params=params(16),
        name="sum_first",
    )(pos, *parts)


def sum_second_kernel(pos, a, b, c, d, *refs):
    outs, t_ref = refs[:-1], refs[-1]
    t_ref[...] = a[...] + b[...].astype(F32) + c[...].astype(F32) + d[...].astype(F32)
    for j, o in enumerate(outs):
        z = (pos[1] + j) % NZ
        o[...] = t_ref[pl.ds(z * 2, 2)].astype(o.dtype)


def sum_second(pos, *parts):
    return pl.pallas_call(
        sum_second_kernel,
        out_shape=[jax.ShapeDtypeStruct((2, 32, 128), BF16 if j else F32) for j in range(NZ)],
        in_specs=smem(1) + vmem(4),
        out_specs=vmem(NZ),
        scratch_shapes=[pltpu.VMEM(parts[0].shape, F32)],
        compiler_params=params(16),
        name="sum_second",
    )(pos, *parts)


def sum_third_kernel(ids, *refs):
    out = refs[-1]
    total = refs[0][...]
    for r in refs[1:-1]:
        total = total + r[...].astype(F32)
    out[0:64, :] = total.reshape(64, 128)
    out[64:72, :] = jnp.full((8, 128), ids[128].astype(F32), F32)


def sum_third(ids, *parts):
    return pl.pallas_call(
        sum_third_kernel,
        out_shape=jax.ShapeDtypeStruct((72, 128), F32),
        in_specs=smem(1) + vmem(NZ),
        out_specs=vmem(1)[0],
        name="sum_third",
    )(ids, *parts)


def finish_kernel(pos, v0, v1, v2, v3, out, t_ref):
    total = (v0[64:65, :] + v1[64:65, :]) + (v2[64:65, :] + v3[64:65, :])
    for j, v in enumerate((v0, v1, v2, v3)):
        q = (pos[0] + j) % NY
        for k in range(2):
            t_ref[k, pl.ds(pl.multiple_of(q * 32, 32), 32), :] = v[k * 32 : k * 32 + 32, :] / total
    for k in range(2):
        out[k] = t_ref[k].T


def finish(pos, *parts):
    return pl.pallas_call(
        finish_kernel,
        out_shape=jax.ShapeDtypeStruct((2, 128, 128), F32),
        in_specs=smem(1) + vmem(4),
        out_specs=vmem(1)[0],
        scratch_shapes=[pltpu.VMEM((2, 128, 128), F32)],
        name="finish",
    )(pos, *parts)


def pack_kernel(frozen_ref, delta_ref, out):
    out[0:128, :] = frozen_ref[...]
    for k in range(2):
        for half in range(2):
            col = (2 * k + half) * 128
            out[128:192, col : col + 128] = delta_ref[k, half * 64 : half * 64 + 64, :]


def pack(frozen, delta_slots):
    return pl.pallas_call(
        pack_kernel,
        out_shape=jax.ShapeDtypeStruct((192, 512), BF16),
        in_specs=vmem(2),
        out_specs=vmem(1)[0],
        name="pack",
    )(frozen, delta_slots)


CHUNK = 8


def build(inverse, w_ref, d_ref, e_ref, chunk):
    for j in range(CHUNK):
        tile = chunk * CHUNK + j
        for col in range(4):
            slot = inverse[tile * 4 + col]
            safe = jnp.maximum(slot, 0)
            lanes = slice(col * 128, col * 128 + 128)
            for half in range(2):
                at = pl.ds(pl.multiple_of((safe % 2 * 2 + half) * 128, 128), 128)
                d = d_ref[safe // 2, :, at].astype(F32)
                d = jnp.where(slot >= 0, d, jnp.zeros_like(d))
                rows = slice(half * 64, half * 64 + 64)
                e_ref[j, rows, lanes] = (w_ref[tile, rows, lanes].astype(F32) + d).astype(BF16)


def products_kernel(inverse, pos, x_ref, cot_ref, all_ref, proj_ref, grad_ref, w_ref, d_ref, m_ref, acc_ref, e0, e1, wsem, dsem):
    step, steps = pl.program_id(0), pl.num_programs(0)
    width = CHUNK * 128
    rows = lax.broadcasted_iota(jnp.int32, acc_ref.shape, 0)

    def weights(n):
        tiles = pl.ds(n * 2 * CHUNK, 2 * CHUNK)
        return pltpu.make_async_copy(all_ref.at[tiles, 0:128, :], w_ref.at[tiles], wsem.at[n])

    @pl.when(step == 0)
    def _():
        deltas = pltpu.make_async_copy(all_ref.at[:, 128:192, :], d_ref, dsem)
        deltas.start()
        weights(0).start()
        g = cot_ref[...]
        m_ref[...] = jnp.where(rows < pos[4], g, jnp.zeros_like(g))
        acc_ref[...] = jnp.zeros_like(acc_ref)
        deltas.wait()
        weights(1).start()
        weights(2).start()
        weights(0).wait()
        build(inverse, w_ref, d_ref, e0, 0)

    def multiply(e_ref, part):
        w = e_ref[...].reshape(width, acc_ref.shape[1])
        lanes = slice(part * width, part * width + width)
        acc_ref[...] += jnp.dot(x_ref[:, lanes], w, preferred_element_type=F32)
        grad_ref[:, lanes] = lax.dot_general(
            m_ref[...], w, (((1,), (1,)), ((), ())), preferred_element_type=F32
        ).astype(BF16)

    build(inverse, w_ref, d_ref, e1, step * 2 + 1)
    multiply(e0, 0)

    @pl.when(step < steps - 1)
    def _():
        @pl.when(step < steps - 3)
        def _():
            weights(step + 3).start()

        weights(step + 1).wait()

    build(inverse, w_ref, d_ref, e0, jnp.minimum(step * 2 + 2, 2 * steps - 1))
    multiply(e1, 1)

    @pl.when(step == steps - 1)
    def _():
        acc = acc_ref[...]
        proj_ref[...] = jnp.where(rows < pos[4], acc, jnp.zeros_like(acc)).astype(BF16)


def products(inverse, pos, x, cot, gathered):
    tokens, width = x.shape
    heads = cot.shape[1]
    wide = 2 * CHUNK * 128
    return pl.pallas_call(
        products_kernel,
        grid=(width // wide,),
        out_shape=[jax.ShapeDtypeStruct((tokens, heads), BF16), jax.ShapeDtypeStruct((tokens, width), BF16)],
        in_specs=smem(2)
        + [
            pl.BlockSpec((tokens, wide), lambda i: (0, i)),
            pl.BlockSpec((tokens, heads), lambda i: (0, 0)),
            pl.BlockSpec(memory_space=pl.ANY),
        ],
        out_specs=[
            pl.BlockSpec((tokens, heads), lambda i: (0, 0)),
            pl.BlockSpec((tokens, wide), lambda i: (0, i)),
        ],
        scratch_shapes=[
            pltpu.VMEM((64, 128, heads), BF16),
            pltpu.VMEM((64, 64, heads), BF16),
            pltpu.VMEM((tokens, heads), BF16),
            pltpu.VMEM((tokens, heads), F32),
            pltpu.VMEM((CHUNK, 128, heads), BF16),
            pltpu.VMEM((CHUNK, 128, heads), BF16),
            pltpu.SemaphoreType.DMA((64 // (2 * CHUNK),)),
            pltpu.SemaphoreType.DMA,
        ],
        compiler_params=params(60),
        cost_estimate=pl.CostEstimate(flops=6_000_000_000, bytes_accessed=25_000_000, transcendentals=0),
        name="products",
    )(inverse, pos, x, cot, gathered)


def per_device(inputs, frozen, cotangent, delta_slots, slot_tile, token_count):
    f = lax.axis_index("fsdp")
    y = lax.axis_index("dp")
    gathered = lax.all_gather(pack(frozen, delta_slots), "fsdp", axis=0)
    here = jnp.zeros((256,), jnp.int32)
    here = lax.dynamic_update_slice(here, slot_tile, (2 * f,))
    here = lax.dynamic_update_slice(here, token_count, (128,))
    ids = lax.psum(here, "fsdp")
    pos = jnp.stack([y, f // 8, f // 2 % 4, f % 2, token_count[0]]).astype(jnp.int32)

    away, mt = grads_away(ids, pos, inputs, cotangent)
    h = grads_home(ids, pos, inputs, mt, other_core(away))
    j = sum_first(pos, h[0], *exchange(h, y_or_x))
    t = sum_second(pos, j[0], *exchange(j, x_or_y))
    q = sum_third(ids, t[0], *exchange(t, along_z))
    owned = finish(pos, q, *[fetch(q, lambda c, d=d: (d, 0, 0, 0)) for d in (1, 2, 3)])

    slots = jnp.arange(128, dtype=jnp.int32)
    tiles = jnp.arange(256, dtype=jnp.int32)
    inverse = jnp.max(jnp.where(ids[None, :128] == tiles[:, None], slots[None, :], -1), axis=1)
    projected, grad_in = products(inverse, pos, inputs, cotangent, gathered)
    return projected, grad_in, owned


def solution(mesh):
    in_specs = (
        P(("dp", "fsdp"), None),
        P("fsdp", None),
        P(("dp", "fsdp"), None),
        P("fsdp", None, None),
        P("fsdp"),
        P(("dp", "fsdp")),
    )
    out_specs = (P(("dp", "fsdp"), None), P(("dp", "fsdp"), None), P("fsdp", None, None))
    return jax.shard_map(per_device, mesh=mesh, in_specs=in_specs, out_specs=out_specs, check_vma=False)
```

```python
import functools

import jax
import jax.numpy as jnp
from jax import lax
from jax.experimental import pallas as pl
from jax.experimental.pallas import tpu as pltpu
from jax.sharding import PartitionSpec as P

NZ, NX, NC, NY = 8, 4, 2, 4
BF16, F32 = jnp.bfloat16, jnp.float32
OWNERS = NZ * NX


def fetch(v, offset):
    pairs = []
    for y in range(NY):
        for z in range(NZ):
            for x in range(NX):
                for c in range(NC):
                    dy, dz, dx, dc = offset(c)
                    near = (((y + dy) % NY * NZ + (z + dz) % NZ) * NX + (x + dx) % NX) * NC + (c ^ dc)
                    pairs.append((near, ((y * NZ + z) * NX + x) * NC + c))
    return lax.ppermute(v, ("dp", "fsdp"), pairs)


def exchange(sent, offset):
    n = len(sent)
    signed = lambda j: j - n if j > n // 2 else j
    return [fetch(sent[n - j], lambda c, j=j: offset(c, signed(j))) for j in range(1, n)]


def other_core(v):
    return fetch(v, lambda c: (0, 0, 0, 1))


def y_or_x(c, d):
    return (d, 0, 0, 0) if c == 0 else (0, 0, d, 0)


def x_or_y(c, d):
    return y_or_x(1 - c, d)


def along_z(c, d):
    return (0, d, 0, 0)


def params(mib):
    return pltpu.CompilerParams(vmem_limit_bytes=mib * 2**20)


def vmem(n):
    return [pl.BlockSpec(memory_space=pltpu.VMEM)] * n


def smem(n):
    return [pl.BlockSpec(memory_space=pltpu.SMEM)] * n


def grad_blocks(ids, core, x_ref, mt_ref, live_ref, emit):
    block, unroll = 128, 4

    def tile_of(i):
        return ids[((i // 2 % NZ * NX + i // (2 * NZ)) * NC + core) * 2 + i % 2]

    def note(i, n):
        live_ref[n] = i
        return n + (tile_of(i) >= 0).astype(jnp.int32)

    n = lax.fori_loop(0, OWNERS * 2, note, 0, unroll=8)
    for p in range(unroll):
        live_ref[n + p] = live_ref[0]

    def one(r, carry):
        for p in range(unroll):
            i = live_ref[r * unroll + p]
            tile = tile_of(i)
            xt = x_ref[:, pl.ds(pl.multiple_of(tile // 4 * block, block), block)]
            mt = mt_ref[pl.ds(pl.multiple_of(tile % 4 * block, block), block), :]
            emit(i, jnp.dot(mt, xt, preferred_element_type=F32))
        return carry

    lax.fori_loop(0, (n + unroll - 1) // unroll, one, 0)


def grads_away_kernel(ids, pos, x_ref, cot_ref, out_ref, mt_ref, live_ref):
    rows = lax.broadcasted_iota(jnp.int32, cot_ref.shape, 0)
    g = cot_ref[...]
    mt_ref[...] = jnp.where(rows < pos[4], g, jnp.zeros_like(g)).T
    out_ref[...] = jnp.zeros_like(out_ref)

    def emit(i, v):
        out_ref[i] = v.astype(BF16)

    grad_blocks(ids, 1 - pos[3], x_ref, mt_ref, live_ref, emit)


def grads_home_kernel(ids, pos, x_ref, mt_ref, r_ref, h0, h1, h2, h3, t_ref, live_ref):
    t_ref[...] = r_ref[...].astype(F32)

    def emit(i, v):
        t_ref[i] = v + r_ref[i].astype(F32)

    grad_blocks(ids, pos[3], x_ref, mt_ref, live_ref, emit)
    @pl.when(pos[3] == 0)
    def _():
        for j, h in enumerate((h0, h1, h2, h3)):
            q = (pos[0] + j) % NY
            h[...] = t_ref[:, pl.ds(pl.multiple_of(q * 32, 32), 32), :].astype(h.dtype)

    @pl.when(pos[3] == 1)
    def _():
        for j, h in enumerate((h0, h1, h2, h3)):
            x = (pos[2] + j) % NX
            h[...] = t_ref[pl.ds(x * 16, 16)].reshape(OWNERS * 2, 32, 128).astype(h.dtype)


def grads_away(ids, pos, x, cot):
    return pl.pallas_call(
        grads_away_kernel,
        out_shape=[
            jax.ShapeDtypeStruct((OWNERS * 2, 128, 128), BF16),
            jax.ShapeDtypeStruct(cot.shape[::-1], BF16),
        ],
        in_specs=smem(2) + vmem(2),
        out_specs=vmem(2),
        scratch_shapes=[pltpu.SMEM((OWNERS * 2 + 8,), jnp.int32)],
        compiler_params=params(32),
        cost_estimate=pl.CostEstimate(flops=3_000_000_000, bytes_accessed=8_000_000, transcendentals=0),
        name="grads_away",
    )(ids, pos, x, cot)


def grads_home(ids, pos, x, mt, r):
    return pl.pallas_call(
        grads_home_kernel,
        out_shape=[jax.ShapeDtypeStruct((OWNERS * 2, 32, 128), d) for d in (F32, BF16, BF16, BF16)],
        in_specs=smem(2) + vmem(3),
        out_specs=vmem(4),
        scratch_shapes=[pltpu.VMEM((OWNERS * 2, 128, 128), F32), pltpu.SMEM((OWNERS * 2 + 8,), jnp.int32)],
        compiler_params=params(32),
        cost_estimate=pl.CostEstimate(flops=3_000_000_000, bytes_accessed=10_000_000, transcendentals=0),
        name="grads_home",
    )(ids, pos, x, mt, r)


def sum_first_kernel(pos, a, b, c, d, j0, j1, j2, j3, t_ref):
    t_ref[...] = a[...] + b[...].astype(F32) + c[...].astype(F32) + d[...].astype(F32)

    @pl.when(pos[3] == 0)
    def _():
        for j, o in enumerate((j0, j1, j2, j3)):
            x = (pos[2] + j) % NX
            o[...] = t_ref[pl.ds(x * 16, 16)].astype(o.dtype)

    @pl.when(pos[3] == 1)
    def _():
        for j, o in enumerate((j0, j1, j2, j3)):
            q = (pos[0] + j) % NY
            for i in range(16):
                o[i] = t_ref[i * 4 + q].astype(o.dtype)


def sum_first(pos, *parts):
    return pl.pallas_call(
        sum_first_kernel,
        out_shape=[jax.ShapeDtypeStruct((16, 32, 128), d) for d in (F32, BF16, BF16, BF16)],
        in_specs=smem(1) + vmem(4),
        out_specs=vmem(4),
        scratch_shapes=[pltpu.VMEM(parts[0].shape, F32)],
        compiler_params=params(16),
        name="sum_first",
    )(pos, *parts)


def sum_second_kernel(pos, a, b, c, d, *refs):
    outs, t_ref = refs[:-1], refs[-1]
    t_ref[...] = a[...] + b[...].astype(F32) + c[...].astype(F32) + d[...].astype(F32)
    for j, o in enumerate(outs):
        z = (pos[1] + j) % NZ
        o[...] = t_ref[pl.ds(z * 2, 2)].astype(o.dtype)


def sum_second(pos, *parts):
    return pl.pallas_call(
        sum_second_kernel,
        out_shape=[jax.ShapeDtypeStruct((2, 32, 128), BF16 if j else F32) for j in range(NZ)],
        in_specs=smem(1) + vmem(4),
        out_specs=vmem(NZ),
        scratch_shapes=[pltpu.VMEM(parts[0].shape, F32)],
        compiler_params=params(16),
        name="sum_second",
    )(pos, *parts)


def sum_third_kernel(ids, *refs):
    out = refs[-1]
    total = refs[0][...]
    for r in refs[1:-1]:
        total = total + r[...].astype(F32)
    out[0:64, :] = total.reshape(64, 128)
    out[64:72, :] = jnp.full((8, 128), ids[128].astype(F32), F32)


def sum_third(ids, *parts):
    return pl.pallas_call(
        sum_third_kernel,
        out_shape=jax.ShapeDtypeStruct((72, 128), F32),
        in_specs=smem(1) + vmem(NZ),
        out_specs=vmem(1)[0],
        name="sum_third",
    )(ids, *parts)


def finish_kernel(pos, v0, v1, v2, v3, out, t_ref):
    total = (v0[64:65, :] + v1[64:65, :]) + (v2[64:65, :] + v3[64:65, :])
    for j, v in enumerate((v0, v1, v2, v3)):
        q = (pos[0] + j) % NY
        for k in range(2):
            t_ref[k, pl.ds(pl.multiple_of(q * 32, 32), 32), :] = v[k * 32 : k * 32 + 32, :] / total
    for k in range(2):
        out[k] = t_ref[k].T


def finish(pos, *parts):
    return pl.pallas_call(
        finish_kernel,
        out_shape=jax.ShapeDtypeStruct((2, 128, 128), F32),
        in_specs=smem(1) + vmem(4),
        out_specs=vmem(1)[0],
        scratch_shapes=[pltpu.VMEM((2, 128, 128), F32)],
        name="finish",
    )(pos, *parts)


def pack_kernel(frozen_ref, delta_ref, out):
    out[0:128, :] = frozen_ref[...]
    for k in range(2):
        for half in range(2):
            col = (2 * k + half) * 128
            out[128:192, col : col + 128] = delta_ref[k, half * 64 : half * 64 + 64, :]


def pack(frozen, delta_slots):
    return pl.pallas_call(
        pack_kernel,
        out_shape=jax.ShapeDtypeStruct((192, 512), BF16),
        in_specs=vmem(2),
        out_specs=vmem(1)[0],
        name="pack",
    )(frozen, delta_slots)


CHUNK = 8


def build(inverse, w_ref, d_ref, e_ref, chunk):
    for j in range(CHUNK):
        tile = chunk * CHUNK + j
        for col in range(4):
            slot = inverse[tile * 4 + col]
            safe = jnp.maximum(slot, 0)
            lanes = slice(col * 128, col * 128 + 128)
            for half in range(2):
                at = pl.ds(pl.multiple_of((safe % 2 * 2 + half) * 128, 128), 128)
                d = d_ref[safe // 2, :, at]
                d = jnp.where(slot >= 0, d, jnp.zeros_like(d))
                rows = slice(half * 64, half * 64 + 64)
                e_ref[j, rows, lanes] = w_ref[tile, rows, lanes] + d


def products_kernel(inverse, pos, x_ref, cot_ref, all_ref, proj_ref, grad_ref, w_ref, d_ref, m_ref, acc_ref, e0, e1, wsem, dsem):
    step, steps = pl.program_id(0), pl.num_programs(0)
    width = CHUNK * 128
    rows = lax.broadcasted_iota(jnp.int32, acc_ref.shape, 0)

    def weights(n):
        tiles = pl.ds(n * 2 * CHUNK, 2 * CHUNK)
        return pltpu.make_async_copy(all_ref.at[tiles, 0:128, :], w_ref.at[tiles], wsem.at[n])

    @pl.when(step == 0)
    def _():
        deltas = pltpu.make_async_copy(all_ref.at[:, 128:192, :], d_ref, dsem)
        deltas.start()
        weights(0).start()
        g = cot_ref[...]
        m_ref[...] = jnp.where(rows < pos[4], g, jnp.zeros_like(g))
        acc_ref[...] = jnp.zeros_like(acc_ref)
        deltas.wait()
        weights(1).start()
        weights(2).start()
        weights(0).wait()
        build(inverse, w_ref, d_ref, e0, 0)

    def multiply(e_ref, part):
        w = e_ref[...].reshape(width, acc_ref.shape[1])
        lanes = slice(part * width, part * width + width)
        acc_ref[...] += jnp.dot(x_ref[:, lanes], w, preferred_element_type=F32)
        grad_ref[:, lanes] = lax.dot_general(
            m_ref[...], w, (((1,), (1,)), ((), ())), preferred_element_type=F32
        ).astype(BF16)

    build(inverse, w_ref, d_ref, e1, step * 2 + 1)
    multiply(e0, 0)

    @pl.when(step < steps - 1)
    def _():
        @pl.when(step < steps - 3)
        def _():
            weights(step + 3).start()

        weights(step + 1).wait()

    build(inverse, w_ref, d_ref, e0, jnp.minimum(step * 2 + 2, 2 * steps - 1))
    multiply(e1, 1)

    @pl.when(step == steps - 1)
    def _():
        acc = acc_ref[...]
        proj_ref[...] = jnp.where(rows < pos[4], acc, jnp.zeros_like(acc)).astype(BF16)


def products(inverse, pos, x, cot, gathered):
    tokens, width = x.shape
    heads = cot.shape[1]
    wide = 2 * CHUNK * 128
    return pl.pallas_call(
        products_kernel,
        grid=(width // wide,),
        out_shape=[jax.ShapeDtypeStruct((tokens, heads), BF16), jax.ShapeDtypeStruct((tokens, width), BF16)],
        in_specs=smem(2)
        + [
            pl.BlockSpec((tokens, wide), lambda i: (0, i)),
            pl.BlockSpec((tokens, heads), lambda i: (0, 0)),
            pl.BlockSpec(memory_space=pl.ANY),
        ],
        out_specs=[
            pl.BlockSpec((tokens, heads), lambda i: (0, 0)),
            pl.BlockSpec((tokens, wide), lambda i: (0, i)),
        ],
        scratch_shapes=[
            pltpu.VMEM((64, 128, heads), BF16),
            pltpu.VMEM((64, 64, heads), BF16),
            pltpu.VMEM((tokens, heads), BF16),
            pltpu.VMEM((tokens, heads), F32),
            pltpu.VMEM((CHUNK, 128, heads), BF16),
            pltpu.VMEM((CHUNK, 128, heads), BF16),
            pltpu.SemaphoreType.DMA((64 // (2 * CHUNK),)),
            pltpu.SemaphoreType.DMA,
        ],
        compiler_params=params(60),
        cost_estimate=pl.CostEstimate(flops=6_000_000_000, bytes_accessed=25_000_000, transcendentals=0),
        name="products",
    )(inverse, pos, x, cot, gathered)


def per_device(inputs, frozen, cotangent, delta_slots, slot_tile, token_count):
    f = lax.axis_index("fsdp")
    y = lax.axis_index("dp")
    gathered = lax.all_gather(pack(frozen, delta_slots), "fsdp", axis=0)
    here = jnp.zeros((256,), jnp.int32)
    here = lax.dynamic_update_slice(here, slot_tile, (2 * f,))
    here = lax.dynamic_update_slice(here, token_count, (128,))
    ids = lax.psum(here, "fsdp")
    pos = jnp.stack([y, f // 8, f // 2 % 4, f % 2, token_count[0]]).astype(jnp.int32)

    away, mt = grads_away(ids, pos, inputs, cotangent)
    h = grads_home(ids, pos, inputs, mt, other_core(away))
    j = sum_first(pos, h[0], *exchange(h, y_or_x))
    t = sum_second(pos, j[0], *exchange(j, x_or_y))
    q = sum_third(ids, t[0], *exchange(t, along_z))
    owned = finish(pos, q, *[fetch(q, lambda c, d=d: (d, 0, 0, 0)) for d in (1, 2, 3)])

    slots = jnp.arange(128, dtype=jnp.int32)
    tiles = jnp.arange(256, dtype=jnp.int32)
    inverse = jnp.max(jnp.where(ids[None, :128] == tiles[:, None], slots[None, :], -1), axis=1)
    projected, grad_in = products(inverse, pos, inputs, cotangent, gathered)
    return projected, grad_in, owned


def solution(mesh):
    in_specs = (
        P(("dp", "fsdp"), None),
        P("fsdp", None),
        P(("dp", "fsdp"), None),
        P("fsdp", None, None),
        P("fsdp"),
        P(("dp", "fsdp")),
    )
    out_specs = (P(("dp", "fsdp"), None), P(("dp", "fsdp"), None), P("fsdp", None, None))
    return jax.shard_map(per_device, mesh=mesh, in_specs=in_specs, out_specs=out_specs, check_vma=False)
```
